32 devices in a mesh: dp: 8 (over y, x, core), mp: 4 (over z).
Axes of the slice: x: 2, y: 2, z: 4, core: 2. Of those that a mesh axis runs over, the one named last changes fastest.
Arguments:
- tokens: bfloat16 [8, 1024, 768], P('dp', 'mp'), may hold values from -6 to 6
- cotangent: bfloat16 [8, 1024, 768], P('dp', 'mp'), may hold values from -6 to 6
- first_gain: bfloat16 [768], P('dp'), may hold values from 0.099609375 to 1.8984375
- first_shift: bfloat16 [768], P('dp'), may hold values from -3 to 3
- w_query: bfloat16 [768, 768], P('dp', 'mp'), may hold values from -0.21875 to 0.21875
- b_query: bfloat16 [12, 64], P('mp', 'dp'), may hold values from -3 to 3
- w_key: bfloat16 [768, 768], P('dp', 'mp'), may hold values from -0.21875 to 0.21875
- w_value: bfloat16 [768, 768], P('dp', 'mp'), may hold values from -0.21875 to 0.21875
- b_value: bfloat16 [12, 64], P('mp', 'dp'), may hold values from -3 to 3
- w_out: bfloat16 [768, 768], P('mp', 'dp'), may hold values from -0.625 to 0.625
- b_out: bfloat16 [768], P('dp'), may hold values from -3 to 3
- second_gain: bfloat16 [768], P('dp'), may hold values from 0.099609375 to 1.8984375
- second_shift: bfloat16 [768], P('dp'), may hold values from -3 to 3
- w_expand: bfloat16 [768, 3072], P('dp', 'mp'), may hold values from -0.21875 to 0.21875
- b_expand: bfloat16 [48, 64], P('mp', 'dp'), may hold values from -3 to 3
- w_reduce: bfloat16 [3072, 768], P('mp', 'dp'), may hold values from -0.15625 to 0.15625
- b_reduce: bfloat16 [768], P('dp'), may hold values from -3 to 3
Outputs:
- result: bfloat16 [8, 1024, 768], P('dp', 'mp')
- grad_tokens: float32 [8, 1024, 768], P('dp', 'mp')
- grad_first_gain: float32 [768], P('dp')
- grad_first_shift: float32 [768], P('dp')
- grad_w_query: float32 [768, 768], P('dp', 'mp')
- grad_b_query: float32 [12, 64], P('mp', 'dp')
- grad_w_key: float32 [768, 768], P('dp', 'mp')
- grad_w_value: float32 [768, 768], P('dp', 'mp')
- grad_b_value: float32 [12, 64], P('mp', 'dp')
- grad_w_out: float32 [768, 768], P('mp', 'dp')
- grad_b_out: float32 [768], P('dp')
- grad_second_gain: float32 [768], P('dp')
- grad_second_shift: float32 [768], P('dp')
- grad_w_expand: float32 [768, 3072], P('dp', 'mp')
- grad_b_expand: float32 [48, 64], P('mp', 'dp')
- grad_w_reduce: float32 [3072, 768], P('mp', 'dp')
- grad_b_reduce: float32 [768], P('dp')
The draws below stay inside these ranges and needn't reach their ends.
All inputs are finite; a program needn't handle non-finite values.
Results may differ from the reference program's by a relative error of at most 0.019.
Values may be sent and summed in bfloat16 or wider, within the bound.
A program may use at most 128 MiB of HBM per device.

```python
import jax
import jax.numpy as jnp
from jax import lax

D = 768
HEADS = 12
HD = 64
FF = 3072
LEN = 1024
SEQS = 8


def raised(array, stream_key, source, target, shards_of, factor):
    def block_of(dim):
        return (jnp.arange(array.shape[dim]) // (array.shape[dim] // shards_of)).reshape((-1,) + (1,) * (array.ndim - 1 - dim))

    one_side = jax.random.permutation(stream_key, shards_of)[block_of(target)]
    other_side = (block_of(target) + shards_of // 2) % shards_of
    return jnp.where((block_of(source) == one_side) | (block_of(source) == other_side), factor * array, array)


def block_scale(stream_key, shape, shards, least, top_value):
    level = 1.0
    for dim, blocks in shards:
        heights = jax.random.uniform(jax.random.fold_in(jax.random.fold_in(stream_key, 6), dim), (blocks,), jnp.float32, least / len(shards), top_value / len(shards))
        level = level * jnp.repeat(jnp.exp(heights), shape[dim] // blocks).reshape((-1,) + (1,) * (len(shape) - 1 - dim))
    return level


def bell_draw(own_key, dims, scale, limit, pieces=(), dtype=jnp.bfloat16):
    level = block_scale(own_key, dims, pieces, -0.22, 0.18) if pieces else 1.0
    array = jax.random.normal(own_key, dims, jnp.float32) * scale * level
    return jnp.minimum(jnp.maximum(array, -limit), limit).astype(dtype)


def bell_draw_with(rng, extent, width, reach, cuts, heavy, held_as=jnp.bfloat16):
    result = width * jax.random.normal(rng, extent, jnp.float32)
    if cuts:
        result = result * block_scale(rng, extent, cuts, -0.22, 0.18)
    return jnp.clip(raised(result, jax.random.fold_in(rng, 3), *heavy), -reach, reach).astype(held_as)


def setup_inputs(seed: int = 0) -> dict:
    seeds = jax.random.split(jax.random.key(seed), 18)
    return {
        "tokens": bell_draw(seeds[0], (SEQS, LEN, D), 1.0, 6.0, ((0, 8), (1, 4))),
        "cotangent": bell_draw_with(seeds[1], (SEQS, LEN, D), 1.0, 6.0, ((0, 8), (1, 4)), (0, 2, 8, 2.0)),
        "first_gain": jnp.clip(1.0 + 0.18 * jax.random.normal(seeds[2], (D,), jnp.float32), 0.099609375, 1.8984375).astype(jnp.bfloat16),
        "first_shift": bell_draw(seeds[3], (D,), 0.5, 3.0, ((0, 8),)),
        "w_query": bell_draw(seeds[4], (D, D), D ** -0.5, 0.21875, ((0, 8), (1, 4))),
        "b_query": bell_draw(seeds[5], (HEADS, HD), 0.5, 3.0, ((0, 4), (1, 8))),
        "w_key": bell_draw(seeds[6], (D, D), D ** -0.5, 0.21875, ((0, 8), (1, 4))),
        "w_value": bell_draw(seeds[7], (D, D), D ** -0.5, 0.21875, ((0, 8), (1, 4))),
        "b_value": bell_draw(seeds[8], (HEADS, HD), 0.5, 3.0, ((0, 4), (1, 8))),
        "w_out": bell_draw(seeds[9], (D, D), (D // 8) ** -0.5, 0.625, ((0, 4), (1, 8))),
        "b_out": bell_draw(seeds[10], (D,), 0.5, 3.0, ((0, 8),)),
        "second_gain": jnp.clip(1.0 + 0.18 * jax.random.normal(seeds[11], (D,), jnp.float32), 0.099609375, 1.8984375).astype(jnp.bfloat16),
        "second_shift": bell_draw(seeds[12], (D,), 0.5, 3.0, ((0, 8),)),
        "w_expand": bell_draw(seeds[13], (D, FF), D ** -0.5, 0.21875, ((0, 8), (1, 4))),
        "b_expand": bell_draw(seeds[14], (FF // HD, HD), 0.5, 3.0, ((0, 4), (1, 8))),
        "w_reduce": bell_draw(seeds[15], (FF, D), (FF // 2) ** -0.5, 0.15625, ((0, 4), (1, 8))),
        "b_reduce": bell_draw(seeds[16], (D,), 0.5, 3.0, ((0, 8),)),
    }


@jax.custom_vjp
def low(v):
    return lax.optimization_barrier(v.astype(jnp.bfloat16)).astype(jnp.float32)

@jax.custom_vjp
def low_back(v):
    return v

def low_keep(v):
    return (low(v), None)

def low_pass(kept, grad):
    return (grad,)

def back_keep(v):
    return (v, None)

def back_low(kept, grad):
    return (low(grad),)
low.defvjp(low_keep, low_pass)
low_back.defvjp(back_keep, back_low)

def norm_rows(v, gain, shift):
    mean = lax.optimization_barrier(jnp.mean(v, axis=-1, keepdims=True))
    centered = v - mean
    spread = lax.optimization_barrier(jnp.mean(centered * centered, axis=-1, keepdims=True))
    return centered * lax.rsqrt(spread + 1e-05) * gain + shift

def gelu_tanh(v):
    return 0.5 * v * (1.0 + jnp.tanh(0.7978845608028654 * (v + 0.044715 * v * v * v)))

def mult(left, right):
    return jnp.dot(left, right, precision=lax.Precision.HIGHEST)

def layer_seq(x, params):
    first_gain, first_shift, w_query, b_query, w_key, w_value, b_value, w_out, b_out, second_gain, second_shift, w_expand, b_expand, w_reduce, b_reduce = params
    scale = HD ** (-0.5)
    normed = low(norm_rows(x, first_gain, first_shift))
    query = low(low_back(mult(normed, w_query) + b_query.reshape(-1)))
    keys = low(low_back(mult(normed, w_key)))
    values = low(low_back(mult(normed, w_value) + b_value.reshape(-1)))
    qhead = query.reshape(LEN, HEADS, HD)
    khead = keys.reshape(LEN, HEADS, HD)
    vhead = values.reshape(LEN, HEADS, HD)
    scores = jnp.einsum('qhd,khd->hqk', qhead, khead, precision=lax.Precision.HIGHEST) * scale
    causal = jnp.arange(LEN)[:, None] >= jnp.arange(LEN)[None, :]
    scores = low_back(jnp.where(causal[None], scores, -1e+30))
    top = lax.optimization_barrier(jnp.max(scores, axis=-1, keepdims=True))
    expo = jnp.exp(scores - top)
    probs = low(expo / lax.optimization_barrier(jnp.sum(expo, axis=-1, keepdims=True)))
    mixed = jnp.einsum('hqk,khd->qhd', probs, vhead, precision=lax.Precision.HIGHEST).reshape(LEN, D)
    mixed = low(low_back(mixed))
    branch = low_back(mult(mixed, w_out) + b_out)
    hidden = x + branch
    second = low(norm_rows(hidden, second_gain, second_shift))
    pre = low_back(mult(second, w_expand) + b_expand.reshape(-1))
    act = low(gelu_tanh(pre))
    branch_two = low_back(mult(act, w_reduce) + b_reduce)
    return hidden + branch_two

def reference(tokens, cotangent, first_gain, first_shift, w_query, b_query, w_key, w_value, b_value, w_out, b_out, second_gain, second_shift, w_expand, b_expand, w_reduce, b_reduce):
    params = tuple((p.astype(jnp.float32) for p in (first_gain, first_shift, w_query, b_query, w_key, w_value, b_value, w_out, b_out, second_gain, second_shift, w_expand, b_expand, w_reduce, b_reduce)))
    inputs = tokens.astype(jnp.float32)
    checked = jax.checkpoint(layer_seq)

    def forward(xs, prm):

        def step(carry, row):
            return (carry, checked(row, prm))
        _, outs = lax.scan(step, jnp.zeros((), jnp.float32), xs)
        return outs
    outs, pull = jax.vjp(forward, inputs, params)
    grad_x, grads = pull(cotangent.astype(jnp.float32))
    return (outs.astype(jnp.bfloat16), grad_x, grads[0], grads[1], grads[2], grads[3], grads[4], grads[5], grads[6], grads[7], grads[8], grads[9], grads[10], grads[11], grads[12], grads[13], grads[14])
```

```python
import jax
import jax.numpy as jnp
from jax import lax
from jax.sharding import PartitionSpec as P

HD = 64
F32 = jnp.float32
BF16 = jnp.bfloat16


def norm_stats(v):
    mean = jnp.mean(v, axis=-1, keepdims=True)
    centered = v - mean
    spread = jnp.mean(centered * centered, axis=-1, keepdims=True)
    rstd = lax.rsqrt(spread + 1e-05)
    return centered * rstd, rstd


def norm_back(grad, xhat, rstd, gain):
    e = grad * gain
    mean_e = jnp.mean(e, axis=-1, keepdims=True)
    mean_ex = jnp.mean(e * xhat, axis=-1, keepdims=True)
    return rstd * (e - mean_e - xhat * mean_ex)


def gelu_tanh(v):
    return 0.5 * v * (1.0 + jnp.tanh(0.7978845608028654 * (v + 0.044715 * v * v * v)))


def dot(a, b):
    return jnp.dot(a, b, preferred_element_type=F32)


def dot_tn(a, b):
    return lax.dot_general(a, b, (((0,), (0,)), ((), ())), preferred_element_type=F32)


def dot_nt(a, b):
    return lax.dot_general(a, b, (((1,), (1,)), ((), ())), preferred_element_type=F32)


def gather_rows(v):
    return lax.all_gather(v, "mp", axis=0, tiled=True)


def scatter_rows(v):
    return lax.psum_scatter(v.astype(BF16), "mp", scatter_dimension=0, tiled=True).astype(F32)


def block_scores(qhead, khead, first, end, scale):
    scores = (
        jnp.einsum("qhd,khd->hqk", qhead[first:end], khead[:end], preferred_element_type=F32)
        * scale
    )
    causal = (first + jnp.arange(end - first))[:, None] >= jnp.arange(end)[None, :]
    return jnp.where(causal[None], scores, -1e30)


def attend_forward(query, keys, values, heads):
    length = query.shape[0]
    block = min(512, length)
    scale = HD ** (-0.5)
    qhead = query.reshape(length, heads, HD)
    khead = keys.reshape(length, heads, HD)
    vhead = values.reshape(length, heads, HD)
    pieces, maxima, totals = ([], [], [])
    for first in range(0, length, block):
        end = first + block
        scores = block_scores(qhead, khead, first, end, scale)
        top = jnp.max(scores, axis=-1, keepdims=True)
        expo = jnp.exp(scores - top)
        total = jnp.sum(expo, axis=-1, keepdims=True)
        probs = (expo / total).astype(BF16)
        mixed = jnp.einsum("hqk,khd->qhd", probs, vhead[:end], preferred_element_type=F32)
        pieces.append(mixed.reshape(block, heads * HD).astype(BF16))
        maxima.append(top)
        totals.append(total)
    return (jnp.concatenate(pieces, 0), maxima, totals)


def attend_backward(query, keys, values, d_mixed, maxima, totals, heads):
    length = query.shape[0]
    block = min(512, length)
    scale = HD ** (-0.5)
    qhead = query.reshape(length, heads, HD)
    khead = keys.reshape(length, heads, HD)
    vhead = values.reshape(length, heads, HD)
    dhead = d_mixed.reshape(length, heads, HD)
    key_acc = jnp.zeros((length, heads, HD), F32)
    value_acc = jnp.zeros((length, heads, HD), F32)
    query_parts = []
    for number, first in enumerate(range(0, length, block)):
        end = first + block
        scores = block_scores(qhead, khead, first, end, scale)
        probs = jnp.exp(scores - maxima[number]) / totals[number]
        d_probs = jnp.einsum(
            "qhd,khd->hqk", dhead[first:end], vhead[:end], preferred_element_type=F32
        )
        inner = jnp.sum(probs * d_probs, axis=-1, keepdims=True)
        d_scores = (probs * (d_probs - inner)).astype(BF16)
        d_query = (
            jnp.einsum("hqk,khd->qhd", d_scores, khead[:end], preferred_element_type=F32) * scale
        )
        query_parts.append(d_query.reshape(block, heads * HD).astype(BF16))
        key_acc = key_acc.at[:end].add(
            jnp.einsum("hqk,qhd->khd", d_scores, qhead[first:end], preferred_element_type=F32)
            * scale
        )
        value_acc = value_acc.at[:end].add(
            jnp.einsum(
                "hqk,qhd->khd", probs.astype(BF16), dhead[first:end], preferred_element_type=F32
            )
        )
    d_keys = key_acc.reshape(length, heads * HD).astype(BF16)
    d_values = value_acc.reshape(length, heads * HD).astype(BF16)
    return (jnp.concatenate(query_parts, 0), d_keys, d_values)


def local(
    tokens,
    cotangent,
    first_gain,
    first_shift,
    w_query,
    b_query,
    w_key,
    w_value,
    b_value,
    w_out,
    b_out,
    second_gain,
    second_shift,
    w_expand,
    b_expand,
    w_reduce,
    b_reduce,
):
    part, ecols = w_query.shape
    fcols = w_expand.shape[1]
    hrows, hcols = b_query.shape
    frows, _ = b_expand.shape
    bias_len = hrows * hcols
    heads_bias = jnp.concatenate([b_query.reshape(-1), b_value.reshape(-1)])
    heads_bias = jnp.pad(heads_bias, (0, part - 2 * bias_len))
    columns = jnp.stack(
        [
            first_gain,
            first_shift,
            b_out,
            second_gain,
            second_shift,
            b_reduce,
            b_expand.reshape(-1),
            heads_bias,
        ],
        axis=1,
    )
    columns = jnp.pad(columns, ((0, 0), (0, 120)))
    token_rows = gather_rows(tokens[0])
    attn_pack = lax.all_gather(
        jnp.concatenate([w_query, w_key, w_value, w_out.T, columns], axis=1), "dp", tiled=True
    )
    mlp_pack = lax.all_gather(
        jnp.concatenate([w_expand, w_reduce.T], axis=1), "dp", tiled=True
    )
    out_rows = gather_rows(cotangent[0])
    width = attn_pack.shape[0]
    ways = width // part
    w_qkv = attn_pack[:, : 3 * ecols]
    w_out_t = attn_pack[:, 3 * ecols : 4 * ecols]
    vectors = attn_pack[:, 4 * ecols : 4 * ecols + 8].astype(F32).T
    gain_one, shift_one, bias_out = vectors[0:1], vectors[1:2], vectors[2:3]
    gain_two, shift_two, bias_red = vectors[3:4], vectors[4:5], vectors[5:6]
    bias_exp = vectors[6].reshape(ways, frows, hcols).transpose(1, 0, 2).reshape(1, -1)
    bias_heads = vectors[7].reshape(ways, part)
    bias_q = bias_heads[:, :bias_len].reshape(ways, hrows, hcols).transpose(1, 0, 2)
    bias_v = bias_heads[:, bias_len : 2 * bias_len].reshape(ways, hrows, hcols)
    bias_v = bias_v.transpose(1, 0, 2)
    bias_qkv = jnp.concatenate(
        [bias_q.reshape(1, -1), jnp.zeros((1, ecols), F32), bias_v.reshape(1, -1)], axis=1
    )
    w_exp = mlp_pack[:, :fcols]
    w_red_t = mlp_pack[:, fcols:]

    xhat_all, _ = norm_stats(token_rows.astype(F32))
    rows_one = (xhat_all * gain_one + shift_one).astype(BF16)
    qkv = (dot(rows_one, w_qkv) + bias_qkv).astype(BF16)
    query, keys, values = qkv[:, :ecols], qkv[:, ecols : 2 * ecols], qkv[:, 2 * ecols :]
    heads = ecols // HD
    mixed, maxima, totals = attend_forward(query, keys, values, heads)
    partial_one = dot_nt(mixed, w_out_t)
    shard = tokens[0].astype(F32)
    hidden = shard + scatter_rows(partial_one) + bias_out
    xhat_two, rstd_two = norm_stats(hidden)
    rows_two = gather_rows((xhat_two * gain_two + shift_two).astype(BF16))
    pre = dot(rows_two, w_exp) + bias_exp
    act_full, back_gelu = jax.vjp(gelu_tanh, pre)
    act = act_full.astype(BF16)
    (d_pre_full,) = back_gelu(dot(out_rows, w_red_t))
    d_pre = d_pre_full.astype(BF16)
    d_second = scatter_rows(dot_nt(d_pre, w_exp))
    partial_two = dot_nt(act, w_red_t)
    result = (hidden + scatter_rows(partial_two) + bias_red).astype(BF16)
    mlp_grads = jnp.concatenate([dot_tn(rows_two, d_pre), dot_tn(out_rows, act)], axis=1)
    mlp_owned = lax.psum_scatter(
        mlp_grads.astype(BF16), "dp", scatter_dimension=0, tiled=True
    ).astype(F32)
    grad_out = cotangent[0].astype(F32)
    grad_bexpand = jnp.sum(d_pre.astype(F32), axis=0)

    grad_gain_two = jnp.sum(d_second * xhat_two, axis=0)
    grad_shift_two = jnp.sum(d_second, axis=0)
    d_hidden = grad_out + norm_back(d_second, xhat_two, rstd_two, gain_two)
    d_hidden_low = d_hidden.astype(BF16)
    hidden_rows = gather_rows(d_hidden_low)
    grad_bout = jnp.sum(d_hidden_low.astype(F32), axis=0)
    grad_breduce = jnp.sum(grad_out, axis=0)
    d_mixed = dot(hidden_rows, w_out_t).astype(BF16)
    d_query, d_keys, d_values = attend_backward(
        query, keys, values, d_mixed, maxima, totals, heads
    )
    d_qkv = jnp.concatenate([d_query, d_keys, d_values], axis=1)
    d_first = scatter_rows(dot_nt(d_qkv, w_qkv))
    attn_grads = jnp.concatenate([dot_tn(rows_one, d_qkv), dot_tn(hidden_rows, mixed)], axis=1)
    attn_owned = lax.psum_scatter(
        attn_grads.astype(BF16), "dp", scatter_dimension=0, tiled=True
    ).astype(F32)
    grad_bq = jnp.sum(d_query.astype(F32), axis=0)
    grad_bv = jnp.sum(d_values.astype(F32), axis=0)

    xhat_one, rstd_one = norm_stats(shard)
    grad_gain_one = jnp.sum(d_first * xhat_one, axis=0)
    grad_shift_one = jnp.sum(d_first, axis=0)
    grad_tokens = d_hidden + norm_back(d_first, xhat_one, rstd_one, gain_one)
    spread = lax.psum(
        jnp.stack(
            [grad_gain_one, grad_shift_one, grad_bout, grad_gain_two, grad_shift_two, grad_breduce]
        ),
        ("dp", "mp"),
    )
    ranks = lax.psum(jnp.concatenate([grad_bq, grad_bv, grad_bexpand]), "dp")
    me = lax.axis_index("dp")
    spread = lax.dynamic_slice_in_dim(spread, me * part, part, 1)
    ranks = lax.dynamic_slice_in_dim(ranks.reshape(-1, HD), me * hcols, hcols, 1)
    return (
        result[None],
        grad_tokens[None],
        spread[0],
        spread[1],
        attn_owned[:, :ecols],
        ranks[:hrows],
        attn_owned[:, ecols : 2 * ecols],
        attn_owned[:, 2 * ecols : 3 * ecols],
        ranks[hrows : 2 * hrows],
        attn_owned[:, 3 * ecols :].T,
        spread[2],
        spread[3],
        spread[4],
        mlp_owned[:, :fcols],
        ranks[2 * hrows :],
        mlp_owned[:, fcols:].T,
        spread[5],
    )


def solution(mesh):
    rows, vec = P("dp", "mp", None), P("dp")
    down, across = P("dp", "mp"), P("mp", "dp")
    params = (
        vec, vec, down, across, down, down, across, across, vec, vec, vec, down, across, across,
        vec,
    )
    return jax.shard_map(
        local,
        mesh=mesh,
        in_specs=(rows, rows) + params,
        out_specs=(rows, rows) + params,
        check_vma=False,
    )
```

```python
import functools

import jax
import jax.numpy as jnp
from jax import lax
from jax.experimental import pallas as pl
from jax.experimental.pallas import tpu as pltpu
from jax.sharding import PartitionSpec as P

HD = 64
F32 = jnp.float32
BF16 = jnp.bfloat16


def norm_stats(v):
    mean = jnp.mean(v, axis=-1, keepdims=True)
    centered = v - mean
    spread = jnp.mean(centered * centered, axis=-1, keepdims=True)
    rstd = lax.rsqrt(spread + 1e-05)
    return centered * rstd, rstd


def norm_back(grad, xhat, rstd, gain):
    e = grad * gain
    mean_e = jnp.mean(e, axis=-1, keepdims=True)
    mean_ex = jnp.mean(e * xhat, axis=-1, keepdims=True)
    return rstd * (e - mean_e - xhat * mean_ex)


def gelu_tanh(v):
    return 0.5 * v * (1.0 + jnp.tanh(0.7978845608028654 * (v + 0.044715 * v * v * v)))


def dot(a, b):
    return jnp.dot(a, b, preferred_element_type=F32)


def dot_tn(a, b):
    return lax.dot_general(a, b, (((0,), (0,)), ((), ())), preferred_element_type=F32)


def dot_nt(a, b):
    return lax.dot_general(a, b, (((1,), (1,)), ((), ())), preferred_element_type=F32)


def greet(groups):
    barrier = pltpu.get_barrier_semaphore()
    for axis, n in groups:
        me = lax.axis_index(axis)
        for k in range(1, n):
            pl.semaphore_signal(
                barrier,
                inc=1,
                device_id={axis: lax.rem(me + k, n)},
                device_id_type=pl.DeviceIdType.MESH,
            )
    pl.semaphore_wait(barrier, sum(n - 1 for _, n in groups))


def push(axis, n, k, src, dst, sends, recvs, base=0):
    copy = pltpu.make_async_remote_copy(
        src_ref=src,
        dst_ref=dst,
        send_sem=sends.at[base + k - 1],
        recv_sem=recvs.at[base + k - 1],
        device_id={axis: lax.rem(lax.axis_index(axis) + k, n)},
        device_id_type=pl.DeviceIdType.MESH,
    )
    copy.start()
    return copy


def send_whole(axis, n, src, slots, sends, recvs, base=0):
    return [push(axis, n, k, src, slots.at[k - 1], sends, recvs, base) for k in range(1, n)]


def send_parts(axis, n, parts, slots, sends, recvs, base=0):
    me = lax.axis_index(axis)
    return [
        push(axis, n, k, parts.at[lax.rem(me + k, n)], slots.at[k - 1], sends, recvs, base)
        for k in range(1, n)
    ]


def send_own(axis, n, src, whole, sends, recvs, base=0):
    me = lax.axis_index(axis)
    return [push(axis, n, k, src, whole.at[me], sends, recvs, base) for k in range(1, n)]


def settle(copies):
    for copy in copies:
        copy.wait()


def total_of(axis, parts, slots):
    total = parts[lax.axis_index(axis)].astype(F32)
    for k in range(slots.shape[0]):
        total = total + slots[k].astype(F32)
    return total


def start_kernel(nz, nd, tok, pack, tok_all, pack_all, zs, zr, ds, dr):
    greet((("mp", nz), ("dp", nd)))
    copies = send_own("mp", nz, tok, tok_all, zs, zr)
    copies += send_own("dp", nd, pack, pack_all, ds, dr)
    tok_all[lax.axis_index("mp")] = tok[...]
    pack_all[lax.axis_index("dp")] = pack[...]
    settle(copies)


def middle_kernel(nz, part, tok, bias, gain, shift, rows, hidden, slots, own, zs, zr):
    greet((("mp", nz),))
    settle(send_parts("mp", nz, part, slots, zs, zr))
    hid = tok[...].astype(F32) + total_of("mp", part, slots) + bias[...]
    hidden[...] = hid
    xhat, _ = norm_stats(hid)
    own[...] = (xhat * gain[...] + shift[...]).astype(BF16)
    copies = send_own("mp", nz, own, rows, zs, zr, nz - 1)
    rows[lax.axis_index("mp")] = own[...]
    settle(copies)


def turn_kernel(nz, part, hidden, cot, gain, rows, d_hidden, vec, slots, own, zs, zr):
    greet((("mp", nz),))
    copies = send_parts("mp", nz, part, slots, zs, zr)
    xhat, rstd = norm_stats(hidden[...])
    grad_out = cot[...].astype(F32)
    settle(copies)
    d_second = total_of("mp", part, slots)
    d_hid = grad_out + norm_back(d_second, xhat, rstd, gain[...])
    own[...] = d_hid.astype(BF16)
    copies = send_own("mp", nz, own, rows, zs, zr, nz - 1)
    d_hidden[...] = d_hid
    rows[lax.axis_index("mp")] = own[...]
    vec[0:1] = jnp.sum(own[...].astype(F32), axis=0, keepdims=True)
    vec[1:2] = jnp.sum(d_second * xhat, axis=0, keepdims=True)
    vec[2:3] = jnp.sum(d_second, axis=0, keepdims=True)
    vec[3:4] = jnp.sum(grad_out, axis=0, keepdims=True)
    settle(copies)


def end_kernel(
    nz, nd, part, grads, tok, gain, d_hidden, vec, ranks,
    grad_tok, owned, sums,
    slots, gslots, mine, zslots, col, dslots, zs, zr, ds, dr,
):
    greet((("mp", nz), ("dp", nd)))
    copies = send_parts("mp", nz, part, slots, zs, zr)
    others = send_parts("dp", nd, grads, gslots, ds, dr)
    xhat, rstd = norm_stats(tok[...].astype(F32))
    settle(copies)
    d_first = total_of("mp", part, slots)
    mine[0:1] = jnp.sum(d_first * xhat, axis=0, keepdims=True)
    mine[1:2] = jnp.sum(d_first, axis=0, keepdims=True)
    mine[2:6] = vec[0:4]
    mine[6:8] = jnp.zeros_like(ranks)
    copies = send_whole("mp", nz, mine, zslots, zs, zr, nz - 1)
    grad_tok[...] = d_hidden[...] + norm_back(d_first, xhat, rstd, gain[...])
    settle(copies)
    total = mine[...]
    for k in range(nz - 1):
        total = total + zslots[k]
    col[0:6] = total[0:6]
    col[6:8] = ranks[...]
    copies = send_whole("dp", nd, col, dslots, ds, dr, nd - 1)
    settle(others)
    owned[...] = total_of("dp", grads, gslots)
    settle(copies)
    total = col[...]
    for k in range(nd - 1):
        total = total + dslots[k]
    sums[...] = total


def exchange(kernel, number, outs, scratch, *args):
    space = pl.BlockSpec(memory_space=pltpu.VMEM)
    return pl.pallas_call(
        kernel,
        out_shape=[jax.ShapeDtypeStruct(*out) for out in outs],
        in_specs=[space] * len(args),
        out_specs=[space] * len(outs),
        scratch_shapes=scratch,
        compiler_params=pltpu.CompilerParams(
            collective_id=number, has_side_effects=True, vmem_limit_bytes=40 * 2**20
        ),
        cost_estimate=pl.CostEstimate(
            flops=25_000_000_000, bytes_accessed=60_000_000, transcendentals=0
        ),
    )(*args)


def sems(count):
    return [pltpu.SemaphoreType.DMA((count,))] * 2


def gather_rows(v):
    return lax.all_gather(v, "mp", axis=0, tiled=True)


def scatter_rows(v):
    return lax.psum_scatter(v.astype(BF16), "mp", scatter_dimension=0, tiled=True).astype(F32)


def block_scores(qhead, khead, first, end, scale):
    scores = (
        jnp.einsum("qhd,khd->hqk", qhead[first:end], khead[:end], preferred_element_type=F32)
        * scale
    )
    causal = (first + jnp.arange(end - first))[:, None] >= jnp.arange(end)[None, :]
    return jnp.where(causal[None], scores, -1e30)


def attend_forward(query, keys, values, heads):
    length = query.shape[0]
    block = min(512, length)
    scale = HD ** (-0.5)
    qhead = query.reshape(length, heads, HD)
    khead = keys.reshape(length, heads, HD)
    vhead = values.reshape(length, heads, HD)
    pieces, maxima, totals = ([], [], [])
    for first in range(0, length, block):
        end = first + block
        scores = block_scores(qhead, khead, first, end, scale)
        top = jnp.max(scores, axis=-1, keepdims=True)
        expo = jnp.exp(scores - top)
        total = jnp.sum(expo, axis=-1, keepdims=True)
        probs = (expo / total).astype(BF16)
        mixed = jnp.einsum("hqk,khd->qhd", probs, vhead[:end], preferred_element_type=F32)
        pieces.append(mixed.reshape(block, heads * HD).astype(BF16))
        maxima.append(top)
        totals.append(total)
    return (jnp.concatenate(pieces, 0), maxima, totals)


def attend_backward(query, keys, values, d_mixed, maxima, totals, heads):
    length = query.shape[0]
    block = min(512, length)
    scale = HD ** (-0.5)
    qhead = query.reshape(length, heads, HD)
    khead = keys.reshape(length, heads, HD)
    vhead = values.reshape(length, heads, HD)
    dhead = d_mixed.reshape(length, heads, HD)
    key_acc = jnp.zeros((length, heads, HD), F32)
    value_acc = jnp.zeros((length, heads, HD), F32)
    query_parts = []
    for number, first in enumerate(range(0, length, block)):
        end = first + block
        scores = block_scores(qhead, khead, first, end, scale)
        probs = jnp.exp(scores - maxima[number]) / totals[number]
        d_probs = jnp.einsum(
            "qhd,khd->hqk", dhead[first:end], vhead[:end], preferred_element_type=F32
        )
        inner = jnp.sum(probs * d_probs, axis=-1, keepdims=True)
        d_scores = (probs * (d_probs - inner)).astype(BF16)
        d_query = (
            jnp.einsum("hqk,khd->qhd", d_scores, khead[:end], preferred_element_type=F32) * scale
        )
        query_parts.append(d_query.reshape(block, heads * HD).astype(BF16))
        key_acc = key_acc.at[:end].add(
            jnp.einsum("hqk,qhd->khd", d_scores, qhead[first:end], preferred_element_type=F32)
            * scale
        )
        value_acc = value_acc.at[:end].add(
            jnp.einsum(
                "hqk,qhd->khd", probs.astype(BF16), dhead[first:end], preferred_element_type=F32
            )
        )
    d_keys = key_acc.reshape(length, heads * HD).astype(BF16)
    d_values = value_acc.reshape(length, heads * HD).astype(BF16)
    return (jnp.concatenate(query_parts, 0), d_keys, d_values)


def local(
    tokens,
    cotangent,
    first_gain,
    first_shift,
    w_query,
    b_query,
    w_key,
    w_value,
    b_value,
    w_out,
    b_out,
    second_gain,
    second_shift,
    w_expand,
    b_expand,
    w_reduce,
    b_reduce,
):
    part, ecols = w_query.shape
    fcols = w_expand.shape[1]
    hrows, hcols = b_query.shape
    frows, _ = b_expand.shape
    bias_len = hrows * hcols
    heads_bias = jnp.concatenate([b_query.reshape(-1), b_value.reshape(-1)])
    heads_bias = jnp.pad(heads_bias, (0, part - 2 * bias_len))
    columns = jnp.stack(
        [
            first_gain,
            first_shift,
            b_out,
            second_gain,
            second_shift,
            b_reduce,
            b_expand.reshape(-1),
            heads_bias,
        ],
        axis=1,
    )
    columns = jnp.pad(columns, ((0, 0), (0, 120)))
    nz, nd = lax.axis_size("mp"), lax.axis_size("dp")
    block, width = tokens.shape[1:]
    attn_own = jnp.concatenate([w_query, w_key, w_value, w_out.T, columns], axis=1)
    token_rows, attn_pack = exchange(
        functools.partial(start_kernel, nz, nd),
        0,
        [((nz, block, width), BF16), ((nd,) + attn_own.shape, BF16)],
        sems(nz - 1) + sems(nd - 1),
        tokens[0],
        attn_own,
    )
    token_rows = token_rows.reshape(nz * block, width)
    attn_pack = attn_pack.reshape(width, -1)
    mlp_pack = lax.all_gather(
        jnp.concatenate([w_expand, w_reduce.T], axis=1), "dp", tiled=True
    )
    out_rows = gather_rows(cotangent[0])
    ways = width // part
    w_qkv = attn_pack[:, : 3 * ecols]
    w_out_t = attn_pack[:, 3 * ecols : 4 * ecols]
    vectors = attn_pack[:, 4 * ecols : 4 * ecols + 8].astype(F32).T
    gain_one, shift_one, bias_out = vectors[0:1], vectors[1:2], vectors[2:3]
    gain_two, shift_two, bias_red = vectors[3:4], vectors[4:5], vectors[5:6]
    bias_exp = vectors[6].reshape(ways, frows, hcols).transpose(1, 0, 2).reshape(1, -1)
    bias_heads = vectors[7].reshape(ways, part)
    bias_q = bias_heads[:, :bias_len].reshape(ways, hrows, hcols).transpose(1, 0, 2)
    bias_v = bias_heads[:, bias_len : 2 * bias_len].reshape(ways, hrows, hcols)
    bias_v = bias_v.transpose(1, 0, 2)
    bias_qkv = jnp.concatenate(
        [bias_q.reshape(1, -1), jnp.zeros((1, ecols), F32), bias_v.reshape(1, -1)], axis=1
    )
    w_exp = mlp_pack[:, :fcols]
    w_red_t = mlp_pack[:, fcols:]

    xhat_all, _ = norm_stats(token_rows.astype(F32))
    rows_one = (xhat_all * gain_one + shift_one).astype(BF16)
    qkv = (dot(rows_one, w_qkv) + bias_qkv).astype(BF16)
    query, keys, values = qkv[:, :ecols], qkv[:, ecols : 2 * ecols], qkv[:, 2 * ecols :]
    heads = ecols // HD
    mixed, maxima, totals = attend_forward(query, keys, values, heads)
    partial_one = dot_nt(mixed, w_out_t)
    rows_shape, own_shape = (nz, block, width), (block, width)
    landing = [pltpu.VMEM((nz - 1, block, width), BF16), pltpu.VMEM(own_shape, BF16)]
    rows_two, hidden = exchange(
        functools.partial(middle_kernel, nz),
        1,
        [(rows_shape, BF16), (own_shape, F32)],
        landing + sems(2 * nz - 2),
        partial_one.astype(BF16).reshape(rows_shape),
        tokens[0],
        bias_out,
        gain_two,
        shift_two,
    )
    rows_two = rows_two.reshape(nz * block, width)
    pre = dot(rows_two, w_exp) + bias_exp
    act_full, back_gelu = jax.vjp(gelu_tanh, pre)
    act = act_full.astype(BF16)
    (d_pre_full,) = back_gelu(dot(out_rows, w_red_t))
    d_pre = d_pre_full.astype(BF16)
    d_second_part = dot_nt(d_pre, w_exp).astype(BF16).reshape(rows_shape)
    hidden_rows, d_hidden, vec = exchange(
        functools.partial(turn_kernel, nz),
        2,
        [(rows_shape, BF16), (own_shape, F32), ((4, width), F32)],
        landing + sems(2 * nz - 2),
        d_second_part,
        hidden,
        cotangent[0],
        gain_two,
    )
    hidden_rows = hidden_rows.reshape(nz * block, width)
    partial_two = dot_nt(act, w_red_t)
    result = (hidden + scatter_rows(partial_two) + bias_red).astype(BF16)
    mlp_grads = jnp.concatenate([dot_tn(rows_two, d_pre), dot_tn(out_rows, act)], axis=1)
    mlp_owned = lax.psum_scatter(
        mlp_grads.astype(BF16), "dp", scatter_dimension=0, tiled=True
    ).astype(F32)
    grad_bexpand = jnp.sum(d_pre.astype(F32), axis=0)

    d_mixed = dot(hidden_rows, w_out_t).astype(BF16)
    d_query, d_keys, d_values = attend_backward(
        query, keys, values, d_mixed, maxima, totals, heads
    )
    d_qkv = jnp.concatenate([d_query, d_keys, d_values], axis=1)
    d_first_part = dot_nt(d_qkv, w_qkv).astype(BF16).reshape(rows_shape)
    attn_grads = jnp.concatenate([dot_tn(rows_one, d_qkv), dot_tn(hidden_rows, mixed)], axis=1)
    grad_bq = jnp.sum(d_query.astype(F32), axis=0)
    grad_bv = jnp.sum(d_values.astype(F32), axis=0)

    ranks = jnp.pad(jnp.concatenate([grad_bq, grad_bv, grad_bexpand]), (0, 2 * width))
    ranks = ranks[: 2 * width].reshape(2, width)
    gparts = attn_grads.astype(BF16).reshape(nd, part, -1)
    grad_tokens, attn_owned, sums = exchange(
        functools.partial(end_kernel, nz, nd),
        3,
        [(own_shape, F32), (gparts.shape[1:], F32), ((8, width), F32)],
        [
            landing[0],
            pltpu.VMEM((nd - 1,) + gparts.shape[1:], BF16),
            pltpu.VMEM((8, width), F32),
            pltpu.VMEM((nz - 1, 8, width), F32),
            pltpu.VMEM((8, width), F32),
            pltpu.VMEM((nd - 1, 8, width), F32),
        ]
        + sems(2 * nz - 2)
        + sems(2 * nd - 2),
        d_first_part,
        gparts,
        tokens[0],
        gain_one,
        d_hidden,
        vec,
        ranks,
    )
    spread = sums[:6]
    count = 2 * hrows + frows
    ranks = sums[6:].reshape(-1)[: count * HD]
    me = lax.axis_index("dp")
    spread = lax.dynamic_slice_in_dim(spread, me * part, part, 1)
    ranks = lax.dynamic_slice_in_dim(ranks.reshape(-1, HD), me * hcols, hcols, 1)
    return (
        result[None],
        grad_tokens[None],
        spread[0],
        spread[1],
        attn_owned[:, :ecols],
        ranks[:hrows],
        attn_owned[:, ecols : 2 * ecols],
        attn_owned[:, 2 * ecols : 3 * ecols],
        ranks[hrows : 2 * hrows],
        attn_owned[:, 3 * ecols :].T,
        spread[2],
        spread[3],
        spread[4],
        mlp_owned[:, :fcols],
        ranks[2 * hrows :],
        mlp_owned[:, fcols:].T,
        spread[5],
    )


def solution(mesh):
    rows, vec = P("dp", "mp", None), P("dp")
    down, across = P("dp", "mp"), P("mp", "dp")
    params = (
        vec, vec, down, across, down, down, across, across, vec, vec, vec, down, across, across,
        vec,
    )
    return jax.shard_map(
        local,
        mesh=mesh,
        in_specs=(rows, rows) + params,
        out_specs=(rows, rows) + params,
        check_vma=False,
    )
```

```python
import functools

import jax
import jax.numpy as jnp
from jax import lax
from jax.experimental import pallas as pl
from jax.experimental.pallas import tpu as pltpu
from jax.sharding import PartitionSpec as P

HD = 64
F32 = jnp.float32
BF16 = jnp.bfloat16


def norm_stats(v):
    mean = jnp.mean(v, axis=-1, keepdims=True)
    centered = v - mean
    spread = jnp.mean(centered * centered, axis=-1, keepdims=True)
    rstd = lax.rsqrt(spread + 1e-05)
    return centered * rstd, rstd


def norm_back(grad, xhat, rstd, gain):
    e = grad * gain
    mean_e = jnp.mean(e, axis=-1, keepdims=True)
    mean_ex = jnp.mean(e * xhat, axis=-1, keepdims=True)
    return rstd * (e - mean_e - xhat * mean_ex)


def gelu_tanh(v):
    return 0.5 * v * (1.0 + jnp.tanh(0.7978845608028654 * (v + 0.044715 * v * v * v)))


def dot(a, b):
    return jnp.dot(a, b, preferred_element_type=F32)


def dot_tn(a, b):
    return lax.dot_general(a, b, (((0,), (0,)), ((), ())), preferred_element_type=F32)


def dot_nt(a, b):
    return lax.dot_general(a, b, (((1,), (1,)), ((), ())), preferred_element_type=F32)


def greet(groups):
    barrier = pltpu.get_barrier_semaphore()
    for axis, n in groups:
        me = lax.axis_index(axis)
        for k in range(1, n):
            pl.semaphore_signal(
                barrier,
                inc=1,
                device_id={axis: lax.rem(me + k, n)},
                device_id_type=pl.DeviceIdType.MESH,
            )
    pl.semaphore_wait(barrier, sum(n - 1 for _, n in groups))


def push(axis, n, k, src, dst, sends, recvs, base=0):
    copy = pltpu.make_async_remote_copy(
        src_ref=src,
        dst_ref=dst,
        send_sem=sends.at[base + k - 1],
        recv_sem=recvs.at[base + k - 1],
        device_id={axis: lax.rem(lax.axis_index(axis) + k, n)},
        device_id_type=pl.DeviceIdType.MESH,
    )
    copy.start()
    return copy


def send_whole(axis, n, src, slots, sends, recvs, base=0):
    return [push(axis, n, k, src, slots.at[k - 1], sends, recvs, base) for k in range(1, n)]


def send_parts(axis, n, parts, slots, sends, recvs, base=0):
    me = lax.axis_index(axis)
    return [
        push(axis, n, k, parts.at[lax.rem(me + k, n)], slots.at[k - 1], sends, recvs, base)
        for k in range(1, n)
    ]


def send_own(axis, n, src, whole, sends, recvs, base=0):
    me = lax.axis_index(axis)
    return [push(axis, n, k, src, whole.at[me], sends, recvs, base) for k in range(1, n)]


def settle(copies):
    for copy in copies:
        copy.wait()


def total_of(axis, parts, slots):
    total = parts[lax.axis_index(axis)].astype(F32)
    for k in range(slots.shape[0]):
        total = total + slots[k].astype(F32)
    return total


def start_kernel(nz, nd, tok, pack, tok_all, pack_all, zs, zr, ds, dr):
    greet((("mp", nz), ("dp", nd)))
    copies = send_own("mp", nz, tok, tok_all, zs, zr)
    copies += send_own("dp", nd, pack, pack_all, ds, dr)
    tok_all[lax.axis_index("mp")] = tok[...]
    pack_all[lax.axis_index("dp")] = pack[...]
    settle(copies)


def middle_kernel(nz, part, tok, bias, gain, shift, rows, hidden, slots, own, zs, zr):
    greet((("mp", nz),))
    settle(send_parts("mp", nz, part, slots, zs, zr))
    hid = tok[...].astype(F32) + total_of("mp", part, slots) + bias[...]
    hidden[...] = hid
    xhat, _ = norm_stats(hid)
    own[...] = (xhat * gain[...] + shift[...]).astype(BF16)
    copies = send_own("mp", nz, own, rows, zs, zr, nz - 1)
    rows[lax.axis_index("mp")] = own[...]
    settle(copies)


def turn_kernel(nz, part, hidden, cot, gain, rows, d_hidden, vec, slots, own, zs, zr):
    greet((("mp", nz),))
    copies = send_parts("mp", nz, part, slots, zs, zr)
    xhat, rstd = norm_stats(hidden[...])
    grad_out = cot[...].astype(F32)
    settle(copies)
    d_second = total_of("mp", part, slots)
    d_hid = grad_out + norm_back(d_second, xhat, rstd, gain[...])
    own[...] = d_hid.astype(BF16)
    copies = send_own("mp", nz, own, rows, zs, zr, nz - 1)
    d_hidden[...] = d_hid
    rows[lax.axis_index("mp")] = own[...]
    vec[0:1] = jnp.sum(own[...].astype(F32), axis=0, keepdims=True)
    vec[1:2] = jnp.sum(d_second * xhat, axis=0, keepdims=True)
    vec[2:3] = jnp.sum(d_second, axis=0, keepdims=True)
    vec[3:4] = jnp.sum(grad_out, axis=0, keepdims=True)
    settle(copies)


def end_kernel(
    nz, nd, part, grads, tok, gain, d_hidden, vec, ranks,
    grad_tok, owned, sums,
    slots, gslots, mine, zslots, col, dslots, zs, zr, ds, dr,
):
    greet((("mp", nz), ("dp", nd)))
    copies = send_parts("mp", nz, part, slots, zs, zr)
    others = send_parts("dp", nd, grads, gslots, ds, dr)
    xhat, rstd = norm_stats(tok[...].astype(F32))
    settle(copies)
    d_first = total_of("mp", part, slots)
    mine[0:1] = jnp.sum(d_first * xhat, axis=0, keepdims=True)
    mine[1:2] = jnp.sum(d_first, axis=0, keepdims=True)
    mine[2:6] = vec[0:4]
    mine[6:8] = jnp.zeros_like(ranks)
    copies = send_whole("mp", nz, mine, zslots, zs, zr, nz - 1)
    grad_tok[...] = d_hidden[...] + norm_back(d_first, xhat, rstd, gain[...])
    settle(copies)
    total = mine[...]
    for k in range(nz - 1):
        total = total + zslots[k]
    col[0:6] = total[0:6]
    col[6:8] = ranks[...]
    copies = send_whole("dp", nd, col, dslots, ds, dr, nd - 1)
    settle(others)
    owned[...] = total_of("dp", grads, gslots)
    settle(copies)
    total = col[...]
    for k in range(nd - 1):
        total = total + dslots[k]
    sums[...] = total


def exchange(kernel, number, outs, scratch, *args):
    space = pl.BlockSpec(memory_space=pltpu.VMEM)
    return pl.pallas_call(
        kernel,
        out_shape=[jax.ShapeDtypeStruct(*out) for out in outs],
        in_specs=[space] * len(args),
        out_specs=[space] * len(outs),
        scratch_shapes=scratch,
        compiler_params=pltpu.CompilerParams(
            collective_id=number, has_side_effects=True, vmem_limit_bytes=40 * 2**20
        ),
        cost_estimate=pl.CostEstimate(
            flops=25_000_000_000, bytes_accessed=60_000_000, transcendentals=0
        ),
    )(*args)


def sems(count):
    return [pltpu.SemaphoreType.DMA((count,))] * 2


def gather_rows(v):
    return lax.all_gather(v, "mp", axis=0, tiled=True)


def scatter_rows(v):
    return lax.psum_scatter(v.astype(BF16), "mp", scatter_dimension=0, tiled=True).astype(F32)


def head_probs(qkv, head, heads, first, block):
    cols = pl.ds(head * HD, HD)
    end = first + block
    query = qkv[first:end, cols] * HD ** (-0.5)
    keys = qkv[:end, pl.ds((heads + head) * HD, HD)]
    scores = dot_nt(query, keys)
    row = first + lax.broadcasted_iota(jnp.int32, scores.shape, 0)
    scores = jnp.where(row >= lax.broadcasted_iota(jnp.int32, scores.shape, 1), scores, -1e30)
    expo = jnp.exp(scores - jnp.max(scores, axis=-1, keepdims=True))
    probs = expo * (1.0 / jnp.sum(expo, axis=-1, keepdims=True))
    return query, keys, probs


def forward_kernel(heads, block, qkv, mixed):
    for head in range(heads):
        for first in range(0, qkv.shape[0], block):
            end = first + block
            _, _, probs = head_probs(qkv, head, heads, first, block)
            values = qkv[:end, pl.ds((2 * heads + head) * HD, HD)]
            mixed[first:end, pl.ds(head * HD, HD)] = dot(probs.astype(BF16), values).astype(BF16)


def backward_kernel(heads, block, qkv, d_mixed, d_qkv, key_sum, value_sum):
    length = qkv.shape[0]
    for head in range(heads):
        for first in reversed(range(0, length, block)):
            end = first + block
            query, keys, probs = head_probs(qkv, head, heads, first, block)
            values = qkv[:end, pl.ds((2 * heads + head) * HD, HD)]
            grad = d_mixed[first:end, pl.ds(head * HD, HD)]
            d_probs = dot_nt(grad, values)
            inner = jnp.sum(probs * d_probs, axis=-1, keepdims=True)
            d_scores = (probs * (d_probs - inner)).astype(BF16)
            d_query = dot(d_scores, keys) * HD ** (-0.5)
            d_qkv[first:end, pl.ds(head * HD, HD)] = d_query.astype(BF16)
            d_keys = dot_tn(d_scores, query)
            d_values = dot_tn(probs.astype(BF16), grad)
            if end == length:
                key_sum[...] = d_keys
                value_sum[...] = d_values
            else:
                key_sum[:end] += d_keys
                value_sum[:end] += d_values
        d_qkv[:, pl.ds((heads + head) * HD, HD)] = key_sum[...].astype(BF16)
        d_qkv[:, pl.ds((2 * heads + head) * HD, HD)] = value_sum[...].astype(BF16)


def attend(kernel, cols, scratch, *args):
    space = pl.BlockSpec(memory_space=pltpu.VMEM)
    return pl.pallas_call(
        kernel,
        out_shape=jax.ShapeDtypeStruct((args[0].shape[0], cols), BF16),
        in_specs=[space] * len(args),
        out_specs=space,
        scratch_shapes=scratch,
        compiler_params=pltpu.CompilerParams(vmem_limit_bytes=40 * 2**20),
        cost_estimate=pl.CostEstimate(
            flops=10_000_000_000, bytes_accessed=20_000_000, transcendentals=0
        ),
    )(*args)


def local(
    tokens,
    cotangent,
    first_gain,
    first_shift,
    w_query,
    b_query,
    w_key,
    w_value,
    b_value,
    w_out,
    b_out,
    second_gain,
    second_shift,
    w_expand,
    b_expand,
    w_reduce,
    b_reduce,
):
    part, ecols = w_query.shape
    fcols = w_expand.shape[1]
    hrows, hcols = b_query.shape
    frows, _ = b_expand.shape
    bias_len = hrows * hcols
    heads_bias = jnp.concatenate([b_query.reshape(-1), b_value.reshape(-1)])
    heads_bias = jnp.pad(heads_bias, (0, part - 2 * bias_len))
    columns = jnp.stack(
        [
            first_gain,
            first_shift,
            b_out,
            second_gain,
            second_shift,
            b_reduce,
            b_expand.reshape(-1),
            heads_bias,
        ],
        axis=1,
    )
    columns = jnp.pad(columns, ((0, 0), (0, 120)))
    nz, nd = lax.axis_size("mp"), lax.axis_size("dp")
    block, width = tokens.shape[1:]
    attn_own = jnp.concatenate([w_query, w_key, w_value, w_out.T, columns], axis=1)
    token_rows, attn_pack = exchange(
        functools.partial(start_kernel, nz, nd),
        0,
        [((nz, block, width), BF16), ((nd,) + attn_own.shape, BF16)],
        sems(nz - 1) + sems(nd - 1),
        tokens[0],
        attn_own,
    )
    token_rows = token_rows.reshape(nz * block, width)
    attn_pack = attn_pack.reshape(width, -1)
    mlp_pack = lax.all_gather(
        jnp.concatenate([w_expand, w_reduce.T], axis=1), "dp", tiled=True
    )
    out_rows = gather_rows(cotangent[0])
    ways = width // part
    w_qkv = attn_pack[:, : 3 * ecols]
    w_out_t = attn_pack[:, 3 * ecols : 4 * ecols]
    vectors = attn_pack[:, 4 * ecols : 4 * ecols + 8].astype(F32).T
    gain_one, shift_one, bias_out = vectors[0:1], vectors[1:2], vectors[2:3]
    gain_two, shift_two, bias_red = vectors[3:4], vectors[4:5], vectors[5:6]
    bias_exp = vectors[6].reshape(ways, frows, hcols).transpose(1, 0, 2).reshape(1, -1)
    bias_heads = vectors[7].reshape(ways, part)
    bias_q = bias_heads[:, :bias_len].reshape(ways, hrows, hcols).transpose(1, 0, 2)
    bias_v = bias_heads[:, bias_len : 2 * bias_len].reshape(ways, hrows, hcols)
    bias_v = bias_v.transpose(1, 0, 2)
    bias_qkv = jnp.concatenate(
        [bias_q.reshape(1, -1), jnp.zeros((1, ecols), F32), bias_v.reshape(1, -1)], axis=1
    )
    w_exp = mlp_pack[:, :fcols]
    w_red_t = mlp_pack[:, fcols:]

    xhat_all, _ = norm_stats(token_rows.astype(F32))
    rows_one = (xhat_all * gain_one + shift_one).astype(BF16)
    qkv = (dot(rows_one, w_qkv) + bias_qkv).astype(BF16)
    heads = ecols // HD
    mixed = attend(functools.partial(forward_kernel, heads, block), ecols, [], qkv)
    partial_one = dot_nt(mixed, w_out_t)
    rows_shape, own_shape = (nz, block, width), (block, width)
    landing = [pltpu.VMEM((nz - 1, block, width), BF16), pltpu.VMEM(own_shape, BF16)]
    rows_two, hidden = exchange(
        functools.partial(middle_kernel, nz),
        1,
        [(rows_shape, BF16), (own_shape, F32)],
        landing + sems(2 * nz - 2),
        partial_one.astype(BF16).reshape(rows_shape),
        tokens[0],
        bias_out,
        gain_two,
        shift_two,
    )
    rows_two = rows_two.reshape(nz * block, width)
    pre = dot(rows_two, w_exp) + bias_exp
    act_full, back_gelu = jax.vjp(gelu_tanh, pre)
    act = act_full.astype(BF16)
    (d_pre_full,) = back_gelu(dot(out_rows, w_red_t))
    d_pre = d_pre_full.astype(BF16)
    d_second_part = dot_nt(d_pre, w_exp).astype(BF16).reshape(rows_shape)
    hidden_rows, d_hidden, vec = exchange(
        functools.partial(turn_kernel, nz),
        2,
        [(rows_shape, BF16), (own_shape, F32), ((4, width), F32)],
        landing + sems(2 * nz - 2),
        d_second_part,
        hidden,
        cotangent[0],
        gain_two,
    )
    hidden_rows = hidden_rows.reshape(nz * block, width)
    partial_two = dot_nt(act, w_red_t)
    result = (hidden + scatter_rows(partial_two) + bias_red).astype(BF16)
    mlp_grads = jnp.concatenate([dot_tn(rows_two, d_pre), dot_tn(out_rows, act)], axis=1)
    mlp_owned = lax.psum_scatter(
        mlp_grads.astype(BF16), "dp", scatter_dimension=0, tiled=True
    ).astype(F32)
    grad_bexpand = jnp.sum(d_pre.astype(F32), axis=0)

    d_mixed = dot(hidden_rows, w_out_t).astype(BF16)
    d_qkv = attend(
        functools.partial(backward_kernel, heads, block),
        3 * ecols,
        [pltpu.VMEM((nz * block, HD), F32)] * 2,
        qkv,
        d_mixed,
    )
    d_first_part = dot_nt(d_qkv, w_qkv).astype(BF16).reshape(rows_shape)
    attn_grads = jnp.concatenate([dot_tn(rows_one, d_qkv), dot_tn(hidden_rows, mixed)], axis=1)
    grad_bqkv = jnp.sum(d_qkv.astype(F32), axis=0)
    grad_bq, grad_bv = grad_bqkv[:ecols], grad_bqkv[2 * ecols :]

    ranks = jnp.pad(jnp.concatenate([grad_bq, grad_bv, grad_bexpand]), (0, 2 * width))
    ranks = ranks[: 2 * width].reshape(2, width)
    gparts = attn_grads.astype(BF16).reshape(nd, part, -1)
    grad_tokens, attn_owned, sums = exchange(
        functools.partial(end_kernel, nz, nd),
        3,
        [(own_shape, F32), (gparts.shape[1:], F32), ((8, width), F32)],
        [
            landing[0],
            pltpu.VMEM((nd - 1,) + gparts.shape[1:], BF16),
            pltpu.VMEM((8, width), F32),
            pltpu.VMEM((nz - 1, 8, width), F32),
            pltpu.VMEM((8, width), F32),
            pltpu.VMEM((nd - 1, 8, width), F32),
        ]
        + sems(2 * nz - 2)
        + sems(2 * nd - 2),
        d_first_part,
        gparts,
        tokens[0],
        gain_one,
        d_hidden,
        vec,
        ranks,
    )
    spread = sums[:6]
    count = 2 * hrows + frows
    ranks = sums[6:].reshape(-1)[: count * HD]
    me = lax.axis_index("dp")
    spread = lax.dynamic_slice_in_dim(spread, me * part, part, 1)
    ranks = lax.dynamic_slice_in_dim(ranks.reshape(-1, HD), me * hcols, hcols, 1)
    return (
        result[None],
        grad_tokens[None],
        spread[0],
        spread[1],
        attn_owned[:, :ecols],
        ranks[:hrows],
        attn_owned[:, ecols : 2 * ecols],
        attn_owned[:, 2 * ecols : 3 * ecols],
        ranks[hrows : 2 * hrows],
        attn_owned[:, 3 * ecols :].T,
        spread[2],
        spread[3],
        spread[4],
        mlp_owned[:, :fcols],
        ranks[2 * hrows :],
        mlp_owned[:, fcols:].T,
        spread[5],
    )


def solution(mesh):
    rows, vec = P("dp", "mp", None), P("dp")
    down, across = P("dp", "mp"), P("mp", "dp")
    params = (
        vec, vec, down, across, down, down, across, across, vec, vec, vec, down, across, across,
        vec,
    )
    return jax.shard_map(
        local,
        mesh=mesh,
        in_specs=(rows, rows) + params,
        out_specs=(rows, rows) + params,
        check_vma=False,
    )
```
